32 devices in a mesh: mode: 4 (over y, x), space: 8 (over z, core).
Axes of the slice: x: 2, y: 2, z: 4, core: 2. Of those that a mesh axis runs over, the one named last changes fastest.
Arguments:
- modes: bfloat16 [64, 16, 64, 128], P('mode', 'space'), may hold values from -1.25 to 1.25
- regions: int32 [16, 64, 128], P('space'), may hold values from 0 to 7
- stiffness: float32 [8], replicated, may hold values from 0.05 to 4
- nonlinear: float32 [8], replicated, may hold values from 0.5 to 2
- plan: int32 [64, 3], P('mode'), may hold values from 0 to 15
Outputs:
- derivatives: float32 [64, 3, 16, 64, 128], P('mode', None, 'space')
The draws below stay inside these ranges and needn't reach their ends.
All inputs are finite; a program needn't handle non-finite values.
Results may differ from the reference program's by a relative error of at most 0.0003.
Values may be sent and summed in bfloat16 or wider, within the bound.
A program may use at most 64 MiB of HBM per device.

```python
import math
import jax
import jax.numpy as jnp
from jax import lax

MODES = 64
REGIONS = 8
PARTNERS = 3
ITERS = 3
NY = 64
NZ = 128
NX = 16
N_MODE = 4


def draw_modes(key, part):
    shape = (MODES, NX, NY, NZ)
    layer = jnp.arange(NX, dtype=jnp.int32)
    level = jnp.where(layer < NX // 2, 0.05, 0.22).astype(jnp.float32)[None, :, None, None]
    values = jax.random.normal(key, shape, jnp.float32)
    return jnp.clip(values * level, -1.25, 1.25).astype(jnp.bfloat16)


def draw_regions(key, part):
    layer = jnp.arange(NX, dtype=jnp.int32)[:, None, None]
    lower = jax.random.randint(key, (NX, NY, NZ), 0, REGIONS // 2, dtype=jnp.int32)
    return jnp.where(layer < NX // 2, lower, lower + REGIONS // 2).astype(jnp.int32)


def draw_stiffness(key, part):
    index = jnp.arange(REGIONS, dtype=jnp.int32)
    unit = jax.random.uniform(key, (REGIONS,), jnp.float32)
    softer = 0.05 * jnp.exp2(unit)
    harder = 2.0 * jnp.exp2(unit)
    return jnp.where(index < REGIONS // 2, softer, harder).astype(jnp.float32)


def touch_ends(drawn, own_key, low, largest):
    dims = drawn.shape
    place = [jax.random.randint(jax.random.fold_in(own_key, axis), (), 0, dims[axis]) for axis in range(len(dims))]
    drawn = drawn.at[tuple(place)].set(low)
    longest = dims.index(max(dims))
    place[longest] = (place[longest] + 1) % dims[longest]
    return drawn.at[tuple(place)].set(largest)


def setup_inputs(seed: int = 0) -> dict:
    streams_of = jax.random.split(jax.random.key(seed), 6)
    modes = draw_modes(jax.random.fold_in(streams_of[5], 71), 0)
    regions = draw_regions(jax.random.fold_in(streams_of[5], 71), 0)
    stiffness = draw_stiffness(jax.random.fold_in(streams_of[5], 71), 0)
    nonlinear = jnp.clip(jnp.exp(jax.random.uniform(streams_of[3], (REGIONS,), jnp.float32, math.log(0.5), math.log(2.0))), 0.5, 2.0)
    plan = touch_ends(jax.random.randint(streams_of[4], (MODES, PARTNERS), 0, MODES // N_MODE), jax.random.fold_in(streams_of[4], 1), 0, (MODES // N_MODE) - 1).astype(jnp.int32)
    return {"modes": modes, "regions": regions, "stiffness": stiffness, "nonlinear": nonlinear, "plan": plan}


mass_shift = 0.5


def laplace(field):
    padded = jnp.pad(field, ((1, 1), (1, 1), (1, 1)))
    beside = padded[2:, 1:-1, 1:-1] + padded[:-2, 1:-1, 1:-1]
    beside = beside + padded[1:-1, 2:, 1:-1] + padded[1:-1, :-2, 1:-1]
    beside = beside + padded[1:-1, 1:-1, 2:] + padded[1:-1, 1:-1, :-2]
    return 6.0 * field - beside


def face_weights(coeff):
    padded = jnp.pad(coeff, ((1, 1), (1, 1), (1, 1)))
    lows_x = 0.5 * (coeff + padded[:-2, 1:-1, 1:-1])
    high_x = 0.5 * (coeff + padded[2:, 1:-1, 1:-1])
    lows_y = 0.5 * (coeff + padded[1:-1, :-2, 1:-1])
    high_y = 0.5 * (coeff + padded[1:-1, 2:, 1:-1])
    lows_z = 0.5 * (coeff + padded[1:-1, 1:-1, :-2])
    high_z = 0.5 * (coeff + padded[1:-1, 1:-1, 2:])
    weights = (lows_x, high_x, lows_y, high_y, lows_z, high_z)
    diag = mass_shift + lows_x + high_x + lows_y + high_y + lows_z + high_z
    return weights, diag


def operate(field, weights, diag):
    lows_x, high_x, lows_y, high_y, lows_z, high_z = weights
    padded = jnp.pad(field, ((0, 0), (1, 1), (1, 1), (1, 1)))
    out = diag * field - lows_x * padded[:, :-2, 1:-1, 1:-1] - high_x * padded[:, 2:, 1:-1, 1:-1]
    out = out - lows_y * padded[:, 1:-1, :-2, 1:-1] - high_y * padded[:, 1:-1, 2:, 1:-1]
    out = out - lows_z * padded[:, 1:-1, 1:-1, :-2] - high_z * padded[:, 1:-1, 1:-1, 2:]
    return out


def reference(modes, regions, stiffness, nonlinear, plan):
    coeff = stiffness[regions]
    cubic = nonlinear[regions]
    weights, diag = face_weights(coeff)
    per_block = MODES // N_MODE

    def one_mode(index):
        own = laplace(lax.dynamic_index_in_dim(modes, index, 0, False).astype(jnp.float32))
        block = index // per_block
        steps = jnp.arange(PARTNERS, dtype=jnp.int32)
        partner = ((block - steps) % N_MODE) * per_block + plan[index]
        fields = jnp.take(modes, partner.astype(jnp.int32), axis=0).astype(jnp.float32)
        rhs = jnp.stack([-laplace(cubic * own * laplace(fields[s])) for s in range(PARTNERS)], 0)
        solution = jnp.zeros_like(rhs)
        residual = rhs
        precond = residual / diag
        direction = precond
        norm_now = jnp.sum(residual * precond, axis=(1, 2, 3))
        for step in range(ITERS):
            image = operate(direction, weights, diag)
            alpha = (norm_now / jnp.sum(direction * image, axis=(1, 2, 3)))[:, None, None, None]
            solution = solution + alpha * direction
            residual = residual - alpha * image
            precond = residual / diag
            norm_next = jnp.sum(residual * precond, axis=(1, 2, 3))
            direction = precond + (norm_next / norm_now)[:, None, None, None] * direction
            norm_now = norm_next
        return solution

    return lax.map(one_mode, jnp.arange(MODES, dtype=jnp.int32))
```

```python
import functools
import jax
import jax.numpy as jnp
from jax import lax
from jax.experimental import pallas as pl
from jax.experimental.pallas import tpu as pltpu
from jax.sharding import PartitionSpec as P

PARTNERS = 3
MASS = 0.5
LEFT = 4
RIGHT = 5
MOMENTS = 6
MESH = pl.DeviceIdType.MESH


def hops_of(reach, slab):
    found = []
    done = 0
    while done < reach:
        take = min(slab, reach - done)
        found.append((done, take))
        done += take
    return found


def ring_barrier(n_mode, n_space):
    mine = lax.axis_index("mode")
    place = lax.axis_index("space")
    barrier = pltpu.get_barrier_semaphore()
    for by in (1, n_space - 1):
        pl.semaphore_signal(barrier, inc=1, device_id=(mine, lax.rem(place + by, n_space)), device_id_type=MESH)
    for by in (1, 2, n_mode - 2, n_mode - 1):
        pl.semaphore_signal(barrier, inc=1, device_id=(lax.rem(mine + by, n_mode), place), device_id_type=MESH)
    pl.semaphore_wait(barrier, 6)


def gather_kernel(n_mode, n_space, slab, modes_ref, ids_ref, ext_ref, idx_ref, own_sem, ms, mr, zs, zr):
    mine = lax.axis_index("mode")
    place = lax.axis_index("space")
    right_hops = hops_of(LEFT, slab)
    left_hops = hops_of(RIGHT, slab)
    ring_barrier(n_mode, n_space)

    def z_copy(group, toward_right, hop):
        done, take = (right_hops if toward_right else left_hops)[hop]
        if toward_right:
            dst = LEFT - done - take
            src = dst + slab
            target = place + 1
        else:
            dst = LEFT + slab + done
            src = dst - slab
            target = place - 1
        if group == PARTNERS:
            src_ref, dst_ref = idx_ref.at[pl.ds(src, take)], idx_ref.at[pl.ds(dst, take)]
            if hop == 0:
                src_ref = ids_ref.at[pl.ds(src - LEFT, take)]
        else:
            src_ref, dst_ref = ext_ref.at[group, :, pl.ds(src, take)], ext_ref.at[group, :, pl.ds(dst, take)]
            if group == 0 and hop == 0:
                src_ref = modes_ref.at[:, pl.ds(src - LEFT, take)]
        side = 0 if toward_right else 1
        return pltpu.make_async_remote_copy(
            src_ref=src_ref,
            dst_ref=dst_ref,
            send_sem=zs.at[group, side, hop],
            recv_sem=zr.at[group, side, hop],
            device_id=(mine, jnp.clip(target, 0, n_space - 1)),
            device_id_type=MESH,
        )

    def sends(toward_right, hop):
        if toward_right:
            return jnp.logical_and(place < n_space - 1, place >= hop)
        return jnp.logical_and(place > 0, place + hop <= n_space - 1)

    def receives(toward_right, hop):
        if toward_right:
            return place >= hop + 1
        return place + hop + 1 <= n_space - 1

    def block_copy(step):
        return pltpu.make_async_remote_copy(
            src_ref=modes_ref,
            dst_ref=ext_ref.at[step, :, pl.ds(LEFT, slab)],
            send_sem=ms.at[step],
            recv_sem=mr.at[step],
            device_id=(lax.rem(mine + step, n_mode), place),
            device_id_type=MESH,
        )

    def each(group, hop, act):
        for toward_right, hops in ((True, right_hops), (False, left_hops)):
            if hop < len(hops):
                act(group, toward_right, hop)

    def start(group, toward_right, hop):
        @pl.when(sends(toward_right, hop))
        def _():
            z_copy(group, toward_right, hop).start()

    def arrive(group, toward_right, hop):
        @pl.when(receives(toward_right, hop))
        def _():
            z_copy(group, toward_right, hop).wait_recv()

    def leave(group, toward_right, hop):
        @pl.when(sends(toward_right, hop))
        def _():
            z_copy(group, toward_right, hop).wait_send()

    depth = max(len(right_hops), len(left_hops))
    own = pltpu.make_async_copy(modes_ref, ext_ref.at[0, :, pl.ds(LEFT, slab)], own_sem.at[0])
    own_ids = pltpu.make_async_copy(ids_ref, idx_ref.at[pl.ds(LEFT, slab)], own_sem.at[1])
    for group in (0, PARTNERS):
        each(group, 0, start)
    for step in range(1, PARTNERS):
        block_copy(step).start()
    own.start()
    own_ids.start()
    for group in [0, PARTNERS] + list(range(1, PARTNERS)):
        if 0 < group < PARTNERS:
            block_copy(group).wait_recv()
            each(group, 0, start)
        for hop in range(depth):
            each(group, hop, arrive)
            if hop + 1 < depth:
                each(group, hop + 1, start)
    own.wait()
    own_ids.wait()
    for step in range(1, PARTNERS):
        block_copy(step).wait_send()
    for group in range(PARTNERS + 1):
        for hop in range(depth):
            each(group, hop, leave)


def gather(n_mode, n_space, modes, ids):
    count, slab, ny, nz = modes.shape
    wide = LEFT + slab + RIGHT
    depth = max(len(hops_of(LEFT, slab)), len(hops_of(RIGHT, slab)))
    return pl.pallas_call(
        functools.partial(gather_kernel, n_mode, n_space, slab),
        out_shape=(
            jax.ShapeDtypeStruct((PARTNERS, count, wide, ny, nz), modes.dtype),
            jax.ShapeDtypeStruct((wide, ny, nz), ids.dtype),
        ),
        in_specs=[pl.BlockSpec(memory_space=pl.ANY)] * 2,
        out_specs=(pl.BlockSpec(memory_space=pl.ANY),) * 2,
        scratch_shapes=[
            pltpu.SemaphoreType.DMA((2,)),
            pltpu.SemaphoreType.DMA((PARTNERS,)),
            pltpu.SemaphoreType.DMA((PARTNERS,)),
            pltpu.SemaphoreType.DMA((PARTNERS + 1, 2, depth)),
            pltpu.SemaphoreType.DMA((PARTNERS + 1, 2, depth)),
        ],
        compiler_params=pltpu.CompilerParams(collective_id=0, has_side_effects=True),
    )(modes, ids)


def shifts(v):
    rows, lanes = v.shape
    return (
        pltpu.roll(v, 1, 0),
        pltpu.roll(v, rows - 1, 0),
        pltpu.roll(v, 1, 1),
        pltpu.roll(v, lanes - 1, 1),
    )


def edge_masks(shape):
    row = lax.broadcasted_iota(jnp.int32, shape, 0)
    lane = lax.broadcasted_iota(jnp.int32, shape, 1)
    return (row > 0, row < shape[0] - 1, lane > 0, lane < shape[1] - 1)


def plane_sum(v, masks):
    total = None
    for moved, keep in zip(shifts(v), masks):
        part = jnp.where(keep, moved, 0.0)
        total = part if total is None else total + part
    return total


def compute_kernel(
    slab, layers,
    plan_ref, stiff_ref, cubic_ref, place_ref, ext_ref, ids_ref,
    basis_ref, mom_ref,
    lap_own, lap_any, coeff, g_ref, dinv, diag_own, scaled, faces,
):
    s = pl.program_id(0)
    count = ext_ref.shape[1]
    shape = ext_ref.shape[-2:]
    wide = LEFT + slab + RIGHT
    base = place_ref[0] * slab - LEFT

    def valid(i):
        at = base + i
        return jnp.logical_and(at >= 0, at < layers)

    @pl.when(s == 0)
    def _():
        masks = edge_masks(shape)
        regions = stiff_ref.shape[0]
        for i in range(1, wide - 1):
            ids = jnp.where(valid(i), ids_ref[i].astype(jnp.float32), 0.0)
            c = jnp.zeros(shape, jnp.float32)
            g = jnp.zeros(shape, jnp.float32)
            for k in range(regions):
                hit = ids == float(k + 1)
                c = jnp.where(hit, stiff_ref[k], c)
                g = jnp.where(hit, cubic_ref[k], g)
            coeff[i - 1] = c
            g_ref[i - 1] = g
        for i in range(2, wide - 2):
            c = coeff[i - 1]
            near = [coeff[i - 2], coeff[i]]
            near += [jnp.where(keep, moved, 0.0) for moved, keep in zip(shifts(c), masks)]
            weights = [0.5 * (c + other) for other in near]
            diag = MASS + weights[0] + weights[1] + weights[2] + weights[3] + weights[4] + weights[5]
            inverse = jnp.where(valid(i), 1.0 / diag, 0.0)
            dinv[i - 2] = inverse
            inside = [weights[0], weights[1]] + [jnp.where(keep, w, 0.0) for w, keep in zip(weights[2:], masks)]
            if 3 <= i < wide - 3:
                for k in range(6):
                    scaled[i - 3, k] = inside[k] * inverse
            if LEFT <= i < LEFT + slab:
                diag_own[i - LEFT] = diag
                faces[i - LEFT, 0] = inside[1]
                faces[i - LEFT, 1] = inside[3]
                faces[i - LEFT, 2] = inside[5]

    def lap_step(j, carry):
        masks = edge_masks(shape)
        below = jnp.where(valid(0), ext_ref[0, j, 0].astype(jnp.float32), 0.0)
        here = jnp.where(valid(1), ext_ref[0, j, 1].astype(jnp.float32), 0.0)
        for i in range(1, wide - 1):
            above = jnp.where(valid(i + 1), ext_ref[0, j, i + 1].astype(jnp.float32), 0.0)
            out = 6.0 * here - (below + above + plane_sum(here, masks))
            lap_any[j, i - 1] = out

            @pl.when(s == 0)
            def _():
                lap_own[j, i - 1] = out * g_ref[i - 1]

            below, here = here, above
        return carry

    lax.fori_loop(0, count, lap_step, 0)

    def apply(v, i):
        below, here, above = v[i - 1], v[i], v[i + 1]
        up, down, west, east = shifts(here)
        w = [scaled[i - 3, k] for k in range(6)]
        return w[0] * below + w[1] * above + w[2] * up + w[3] * down + w[4] * west + w[5] * east

    def field_step(a, carry):
        masks = edge_masks(shape)
        j = plan_ref[a, s]
        prod, v0, v1, v2 = {}, {}, {}, {}
        sums = [None] * MOMENTS

        def add(k, value):
            sums[k] = value if sums[k] is None else sums[k] + value

        def own(i):
            return LEFT <= i < LEFT + slab

        for i in range(1, wide + 5):
            if i < wide - 1:
                prod[i] = lap_own[a, i - 1] * lap_any[j, i - 1]
            e = i - 1
            if 2 <= e < wide - 2:
                rhs = prod[e - 1] + prod[e + 1] + plane_sum(prod[e], masks) - 6.0 * prod[e]
                v0[e] = rhs * dinv[e - 2]
                if own(e):
                    basis_ref[0, a, e - LEFT] = v0[e]
                    add(0, rhs * v0[e])
            e = i - 2
            if 3 <= e < wide - 3:
                v1[e] = apply(v0, e)
                if own(e):
                    basis_ref[1, a, e - LEFT] = v1[e]
                    heavy = diag_own[e - LEFT] * v1[e]
                    add(1, heavy * v0[e])
                    add(2, heavy * v1[e])
            e = i - 3
            if LEFT <= e < wide - 4:
                v2[e] = apply(v1, e)
                if own(e):
                    basis_ref[2, a, e - LEFT] = v2[e]
                    heavy = diag_own[e - LEFT] * v2[e]
                    add(3, heavy * v1[e])
                    add(4, heavy * v2[e])
            e = i - 4
            if own(e):
                here = v2[e]
                up, down, west, east = shifts(here)
                flow = faces[e - LEFT, 0] * v2[e + 1] + faces[e - LEFT, 1] * down + faces[e - LEFT, 2] * east
                add(5, 2.0 * (flow * here))
        for k in range(MOMENTS):
            mom_ref[0, a, k] = jnp.sum(sums[k], axis=0)
        return carry

    lax.fori_loop(0, count, field_step, 0)


def compute(n_space, plan, stiffness, nonlinear, place, ext, ids, slab):
    _, count, wide, ny, nz = ext.shape
    plane = (ny, nz)
    smem = pl.BlockSpec(memory_space=pltpu.SMEM)
    return pl.pallas_call(
        functools.partial(compute_kernel, slab, n_space * slab),
        grid=(PARTNERS,),
        out_shape=(
            jax.ShapeDtypeStruct((PARTNERS, PARTNERS * count, slab, ny, nz), jnp.float32),
            jax.ShapeDtypeStruct((PARTNERS, count, MOMENTS, nz), jnp.float32),
        ),
        in_specs=[
            smem, smem, smem, smem,
            pl.BlockSpec((1, count, wide, ny, nz), lambda s: (s, 0, 0, 0, 0)),
            pl.BlockSpec((wide, ny, nz), lambda s: (0, 0, 0)),
        ],
        out_specs=(
            pl.BlockSpec((PARTNERS, count, slab, ny, nz), lambda s: (0, s, 0, 0, 0)),
            pl.BlockSpec((1, count, MOMENTS, nz), lambda s: (s, 0, 0, 0)),
        ),
        scratch_shapes=[
            pltpu.VMEM((count, wide - 2) + plane, jnp.float32),
            pltpu.VMEM((count, wide - 2) + plane, jnp.float32),
            pltpu.VMEM((wide - 2,) + plane, jnp.float32),
            pltpu.VMEM((wide - 2,) + plane, jnp.float32),
            pltpu.VMEM((wide - 4,) + plane, jnp.float32),
            pltpu.VMEM((slab,) + plane, jnp.float32),
            pltpu.VMEM((wide - 6, 6) + plane, jnp.float32),
            pltpu.VMEM((slab, 3) + plane, jnp.float32),
        ],
        compiler_params=pltpu.CompilerParams(vmem_limit_bytes=48 * 1024 * 1024),
    )(plan, stiffness, nonlinear, place, ext, ids)


def coefficients(m):
    zero = jnp.zeros_like(m[0])
    one = jnp.ones_like(m[0])

    def form(left, right, at):
        total = zero
        for i in range(3):
            for j in range(3):
                if left[i] is not None and right[j] is not None:
                    total = total + left[i] * right[j] * m[i + j + at]
        return total

    z = [one, None, None]
    p = [one, None, None]
    x = [zero, zero, zero]
    rz = m[0]
    for step in range(3):
        alpha = rz / (form(p, p, 0) - form(p, p, 1))
        x = [x[i] if p[i] is None else x[i] + alpha * p[i] for i in range(3)]
        if step == 2:
            break
        old = z
        z = []
        for i in range(3):
            change = zero if p[i] is None else p[i]
            if i > 0 and p[i - 1] is not None:
                change = change - p[i - 1]
            if i > step + 1:
                z.append(None)
            else:
                z.append((zero if old[i] is None else old[i]) - alpha * change)
        new = form(z, z, 0)
        ratio = new / rz
        p = [None if z[i] is None else z[i] + (ratio * p[i] if p[i] is not None else 0.0) for i in range(3)]
        rz = new
    return x


def reduce_kernel(n_space, mom_ref, out_ref, slots, ss, rs):
    mine = lax.axis_index("mode")
    place = lax.axis_index("space")
    barrier = pltpu.get_barrier_semaphore()
    for by in range(1, n_space):
        pl.semaphore_signal(barrier, inc=1, device_id=(mine, lax.rem(place + by, n_space)), device_id_type=MESH)
    pl.semaphore_wait(barrier, n_space - 1)
    copies = []
    for by in range(1, n_space):
        copy = pltpu.make_async_remote_copy(
            src_ref=mom_ref,
            dst_ref=slots.at[by],
            send_sem=ss.at[by],
            recv_sem=rs.at[by],
            device_id=(mine, lax.rem(place + by, n_space)),
            device_id_type=MESH,
        )
        copy.start()
        copies.append(copy)
    total = mom_ref[...]
    for by in range(1, n_space):
        copies[by - 1].wait_recv()
        total = total + slots[by]
    m = [total[k : k + 1] for k in range(MOMENTS)]
    found = coefficients(m)
    out_ref[...] = jnp.concatenate(found + [jnp.zeros_like(total[: total.shape[0] - 3])], 0)
    for copy in copies:
        copy.wait_send()


def reduce_moments(n_space, moments):
    return pl.pallas_call(
        functools.partial(reduce_kernel, n_space),
        out_shape=jax.ShapeDtypeStruct(moments.shape, jnp.float32),
        in_specs=[pl.BlockSpec(memory_space=pltpu.VMEM)],
        out_specs=pl.BlockSpec(memory_space=pltpu.VMEM),
        scratch_shapes=[
            pltpu.VMEM((n_space,) + moments.shape, jnp.float32),
            pltpu.SemaphoreType.DMA((n_space,)),
            pltpu.SemaphoreType.DMA((n_space,)),
        ],
        compiler_params=pltpu.CompilerParams(collective_id=1, has_side_effects=True),
    )(moments)


def shards(n_mode, n_space, modes, regions, stiffness, nonlinear, plan):
    count, slab, ny, nz = modes.shape
    place = lax.axis_index("space").astype(jnp.int32)[None]
    ids = (regions + 1).astype(jnp.bfloat16)
    ext, idx = gather(n_mode, n_space, modes, ids)
    basis, moments = compute(n_space, plan, stiffness, nonlinear, place, ext, idx, slab)
    fields = PARTNERS * count
    sums = jnp.sum(moments, -1).reshape(fields, MOMENTS).T
    sums = jnp.pad(sums, ((0, 8 - MOMENTS), (0, 128 - fields)))
    found = reduce_moments(n_space, sums)[:3, :fields, None, None, None]
    x = found[0] * basis[0] + found[1] * basis[1] + found[2] * basis[2]
    return jnp.swapaxes(x.reshape((PARTNERS, count, slab, ny, nz)), 0, 1)


def solution(mesh):
    return jax.shard_map(
        functools.partial(shards, mesh.shape["mode"], mesh.shape["space"]),
        mesh=mesh,
        in_specs=(
            P("mode", "space", None, None),
            P("space", None, None),
            P(),
            P(),
            P("mode", None),
        ),
        out_specs=P("mode", None, "space", None, None),
        check_vma=False,
    )
```

```python
import functools
import jax
import jax.numpy as jnp
from jax import lax
from jax.experimental import pallas as pl
from jax.experimental.pallas import tpu as pltpu
from jax.sharding import PartitionSpec as P

PARTNERS = 3
MASS = 0.5
LEFT = 4
RIGHT = 5
MOMENTS = 6
MESH = pl.DeviceIdType.MESH


def hops_of(reach, slab):
    found = []
    done = 0
    while done < reach:
        take = min(slab, reach - done)
        found.append((done, take))
        done += take
    return found


def shifts(v):
    rows, lanes = v.shape
    return (
        pltpu.roll(v, 1, 0),
        pltpu.roll(v, rows - 1, 0),
        pltpu.roll(v, 1, 1),
        pltpu.roll(v, lanes - 1, 1),
    )


def edge_masks(shape):
    row = lax.broadcasted_iota(jnp.int32, shape, 0)
    lane = lax.broadcasted_iota(jnp.int32, shape, 1)
    return (row > 0, row < shape[0] - 1, lane > 0, lane < shape[1] - 1)


def stencil_matrix(size, middle):
    row = lax.broadcasted_iota(jnp.int32, (size, size), 0)
    column = lax.broadcasted_iota(jnp.int32, (size, size), 1)
    beside = jnp.logical_or(row == column + 1, column == row + 1)
    return jnp.where(row == column, middle, jnp.where(beside, -1.0, 0.0)).astype(jnp.bfloat16)


def dot(left, right):
    return jnp.dot(left, right, preferred_element_type=jnp.float32)


def kernel(
    n_mode, n_space, count, slab,
    plan_ref, stiff_ref, cubic_ref, modes_ref, ids_ref,
    out_ref,
    ext_ref, idx_ref, lap_own, lap_any, coeff, g_ref, dinv, diag_own, scaled, faces,
    lanes_mat, rows_mat, basis_ref, mom_ref, sums_ref, slots, coef_ref,
    own_sem, ms, mr, zs, zr, ss, rs,
):
    mine = lax.axis_index("mode")
    place = lax.axis_index("space")
    shape = ext_ref.shape[-2:]
    wide = LEFT + slab + RIGHT
    layers = n_space * slab
    base = place * slab - LEFT
    right_hops = hops_of(LEFT, slab)
    left_hops = hops_of(RIGHT, slab)

    barrier = pltpu.get_barrier_semaphore()
    for by in range(1, n_space):
        pl.semaphore_signal(barrier, inc=1, device_id=(mine, lax.rem(place + by, n_space)), device_id_type=MESH)
    for by in (1, 2, n_mode - 2, n_mode - 1):
        pl.semaphore_signal(barrier, inc=1, device_id=(lax.rem(mine + by, n_mode), place), device_id_type=MESH)
    pl.semaphore_wait(barrier, n_space - 1 + 4)

    def z_copy(group, toward_right, hop):
        done, take = (right_hops if toward_right else left_hops)[hop]
        if toward_right:
            dst = LEFT - done - take
            src = dst + slab
            target = place + 1
        else:
            dst = LEFT + slab + done
            src = dst - slab
            target = place - 1
        if group == PARTNERS:
            src_ref, dst_ref = idx_ref.at[pl.ds(src, take)], idx_ref.at[pl.ds(dst, take)]
            if hop == 0:
                src_ref = ids_ref.at[pl.ds(src - LEFT, take)]
        else:
            src_ref, dst_ref = ext_ref.at[group, :, pl.ds(src, take)], ext_ref.at[group, :, pl.ds(dst, take)]
            if group == 0 and hop == 0:
                src_ref = modes_ref.at[:, pl.ds(src - LEFT, take)]
        side = 0 if toward_right else 1
        return pltpu.make_async_remote_copy(
            src_ref=src_ref,
            dst_ref=dst_ref,
            send_sem=zs.at[group, side, hop],
            recv_sem=zr.at[group, side, hop],
            device_id=(mine, jnp.clip(target, 0, n_space - 1)),
            device_id_type=MESH,
        )

    def sends(toward_right, hop):
        if toward_right:
            return jnp.logical_and(place < n_space - 1, place >= hop)
        return jnp.logical_and(place > 0, place + hop <= n_space - 1)

    def receives(toward_right, hop):
        if toward_right:
            return place >= hop + 1
        return place + hop + 1 <= n_space - 1

    def block_copy(step):
        return pltpu.make_async_remote_copy(
            src_ref=modes_ref,
            dst_ref=ext_ref.at[step, :, pl.ds(LEFT, slab)],
            send_sem=ms.at[step],
            recv_sem=mr.at[step],
            device_id=(lax.rem(mine + step, n_mode), place),
            device_id_type=MESH,
        )

    def each(group, hop, act):
        for toward_right, hops in ((True, right_hops), (False, left_hops)):
            if hop < len(hops):
                act(group, toward_right, hop)

    def start(group, toward_right, hop):
        @pl.when(sends(toward_right, hop))
        def _():
            z_copy(group, toward_right, hop).start()

    def arrive(group, toward_right, hop):
        @pl.when(receives(toward_right, hop))
        def _():
            z_copy(group, toward_right, hop).wait_recv()

    def leave(group, toward_right, hop):
        @pl.when(sends(toward_right, hop))
        def _():
            z_copy(group, toward_right, hop).wait_send()

    depth = max(len(right_hops), len(left_hops))

    def advance(group, hop):
        each(group, hop, arrive)
        if hop + 1 < depth:
            each(group, hop + 1, start)

    def open_block(group):
        block_copy(group).wait_recv()
        each(group, 0, start)

    def set_up():
        masks = edge_masks(shape)
        regions = stiff_ref.shape[0]
        for i in range(1, wide - 1):
            ids = idx_ref[i].astype(jnp.float32)
            c = jnp.zeros(shape, jnp.float32)
            g = jnp.zeros(shape, jnp.float32)
            for k in range(regions):
                hit = ids == float(k + 1)
                c = jnp.where(hit, stiff_ref[k], c)
                g = jnp.where(hit, cubic_ref[k], g)
            coeff[i - 1] = c
            g_ref[i - 1] = g
        for i in range(2, wide - 2):
            c = coeff[i - 1]
            near = [coeff[i - 2], coeff[i]]
            near += [jnp.where(keep, moved, 0.0) for moved, keep in zip(shifts(c), masks)]
            weights = [0.5 * (c + other) for other in near]
            diag = MASS + weights[0] + weights[1] + weights[2] + weights[3] + weights[4] + weights[5]
            inside_grid = jnp.logical_and(base + i >= 0, base + i < layers).astype(jnp.float32)
            inverse = inside_grid / diag
            dinv[i - 2] = inverse
            inside = [weights[0], weights[1]] + [jnp.where(keep, w, 0.0) for w, keep in zip(weights[2:], masks)]
            if 3 <= i < wide - 3:
                for k in range(6):
                    scaled[i - 3, k] = inside[k] * inverse
            if LEFT <= i < LEFT + slab:
                diag_own[i - LEFT] = diag
                faces[i - LEFT, 0] = inside[1]
                faces[i - LEFT, 1] = inside[3]
                faces[i - LEFT, 2] = inside[5]

    def lap_loop(group):
        def lap_step(j, carry):
            across = lanes_mat[: shape[1]]
            along = rows_mat[:, : shape[0]]
            raw = [ext_ref[group, j, i] for i in range(wide)]
            plain = [v.astype(jnp.float32) for v in raw]
            for i in range(1, wide - 1):
                out = dot(raw[i], across) + dot(along, raw[i]) - (plain[i - 1] + plain[i + 1])
                lap_any[j, i - 1] = out
                if group == 0:
                    lap_own[j, i - 1] = out * g_ref[i - 1]
            return carry

        lax.fori_loop(0, count, lap_step, 0)

    def apply(v, i):
        below, here, above = v[i - 1], v[i], v[i + 1]
        up, down, west, east = shifts(here)
        w = [scaled[i - 3, k] for k in range(6)]
        return w[0] * below + w[1] * above + w[2] * up + w[3] * down + w[4] * west + w[5] * east

    def field_loop(s, first, last):
        def field_step(a, carry):
            j = plan_ref[a, s]
            prod, v0, v1, v2 = {}, {}, {}, {}
            sums = [None] * MOMENTS

            def add(k, value):
                sums[k] = value if sums[k] is None else sums[k] + value

            def own(i):
                return LEFT <= i < LEFT + slab

            for i in range(1, wide + 5):
                if i < wide - 1:
                    prod[i] = lap_own[a, i - 1] * lap_any[j, i - 1]
                e = i - 1
                if 2 <= e < wide - 2:
                    high = prod[e].astype(jnp.bfloat16)
                    low = (prod[e] - high.astype(jnp.float32)).astype(jnp.bfloat16)
                    rhs = prod[e - 1] + prod[e + 1]
                    rhs = rhs - dot(jnp.concatenate([high, low], 1), lanes_mat[...])
                    rhs = rhs - dot(rows_mat[...], jnp.concatenate([high, low], 0))
                    v0[e] = rhs * dinv[e - 2]
                    if own(e):
                        basis_ref[0, s, a, e - LEFT] = v0[e]
                        add(0, rhs * v0[e])
                e = i - 2
                if 3 <= e < wide - 3:
                    v1[e] = apply(v0, e)
                    if own(e):
                        basis_ref[1, s, a, e - LEFT] = v1[e]
                        heavy = diag_own[e - LEFT] * v1[e]
                        add(1, heavy * v0[e])
                        add(2, heavy * v1[e])
                e = i - 3
                if LEFT <= e < wide - 4:
                    v2[e] = apply(v1, e)
                    if own(e):
                        basis_ref[2, s, a, e - LEFT] = v2[e]
                        heavy = diag_own[e - LEFT] * v2[e]
                        add(3, heavy * v1[e])
                        add(4, heavy * v2[e])
                e = i - 4
                if own(e):
                    here = v2[e]
                    up, down, west, east = shifts(here)
                    flow = faces[e - LEFT, 0] * v2[e + 1] + faces[e - LEFT, 1] * down + faces[e - LEFT, 2] * east
                    add(5, 2.0 * (flow * here))
            for k in range(MOMENTS):
                mom_ref[k, pl.ds(s * count + a, 1), :] = jnp.sum(sums[k], axis=0, keepdims=True)
            return carry

        lax.fori_loop(first, last, field_step, 0)

    own = pltpu.make_async_copy(modes_ref, ext_ref.at[0, :, pl.ds(LEFT, slab)], own_sem.at[0])
    own_ids = pltpu.make_async_copy(ids_ref, idx_ref.at[pl.ds(LEFT, slab)], own_sem.at[1])
    for group in (0, PARTNERS):
        each(group, 0, start)
    for step in range(1, PARTNERS):
        block_copy(step).start()
    own.start()
    own_ids.start()
    for i in list(range(LEFT)) + list(range(LEFT + slab, wide)):
        @pl.when(base + i < 0 if i < LEFT else base + i >= layers)
        def _():
            idx_ref[i] = jnp.zeros(shape, idx_ref.dtype)

            def clear(j, carry):
                for group in range(PARTNERS):
                    ext_ref[group, j, i] = jnp.zeros(shape, ext_ref.dtype)
                return carry

            lax.fori_loop(0, count, clear, 0)
    lanes_mat[...] = jnp.concatenate([stencil_matrix(shape[1], 6.0)] * 2, 0)
    rows_mat[...] = jnp.concatenate([stencil_matrix(shape[0], 0.0)] * 2, 1)
    mom_ref[...] = jnp.zeros_like(mom_ref)
    own.wait()
    own_ids.wait()

    for hop in range(depth):
        advance(PARTNERS, hop)
        advance(0, hop)
        if hop == min(1, depth - 1):
            open_block(1)
    set_up()
    lap_loop(0)
    half = count // 2
    advance(1, 0)
    open_block(2)
    field_loop(0, 0, half)
    for hop in range(1, depth):
        advance(1, hop)
        advance(2, hop - 1)
        if hop == 1:
            field_loop(0, half, count)
    lap_loop(1)
    field_loop(1, 0, count)
    advance(2, depth - 1)
    lap_loop(2)
    field_loop(2, 0, count)

    ones = jnp.ones((8, shape[1]), jnp.float32)
    rows = []
    for k in range(MOMENTS):
        rows.append(
            lax.dot_general(
                ones, mom_ref[k], (((1,), (1,)), ((), ())),
                precision=lax.Precision.HIGHEST, preferred_element_type=jnp.float32,
            )[:1]
        )
    rows.append(jnp.zeros((8 - MOMENTS, mom_ref.shape[1]), jnp.float32))
    sums_ref[...] = jnp.concatenate(rows, 0)
    copies = []
    for by in range(1, n_space):
        copy = pltpu.make_async_remote_copy(
            src_ref=sums_ref,
            dst_ref=slots.at[by],
            send_sem=ss.at[by],
            recv_sem=rs.at[by],
            device_id=(mine, lax.rem(place + by, n_space)),
            device_id_type=MESH,
        )
        copy.start()
        copies.append(copy)
    total = sums_ref[...]
    for by in range(1, n_space):
        copies[by - 1].wait_recv()
        total = total + slots[by]
    found = coefficients([total[k : k + 1] for k in range(MOMENTS)])
    for k in range(3):
        coef_ref[k] = jnp.transpose(jnp.broadcast_to(found[k], coef_ref.shape[1:]))

    for s in range(PARTNERS):
        def combine(a, carry):
            c = [coef_ref[k, pl.ds(s * count + a, 1), :] for k in range(3)]
            for i in range(slab):
                out_ref[a, s, i] = (
                    c[0] * basis_ref[0, s, a, i] + c[1] * basis_ref[1, s, a, i] + c[2] * basis_ref[2, s, a, i]
                )
            return carry

        lax.fori_loop(0, count, combine, 0)

    for copy in copies:
        copy.wait_send()
    for step in range(1, PARTNERS):
        block_copy(step).wait_send()
    for group in range(PARTNERS + 1):
        for hop in range(depth):
            each(group, hop, leave)


def shards(n_mode, n_space, modes, regions, stiffness, nonlinear, plan):
    count, slab, ny, nz = modes.shape
    ids = (regions + 1).astype(jnp.bfloat16)
    wide = LEFT + slab + RIGHT
    depth = max(len(hops_of(LEFT, slab)), len(hops_of(RIGHT, slab)))
    padded = -(-PARTNERS * count // nz) * nz
    plane = (ny, nz)
    smem = pl.BlockSpec(memory_space=pltpu.SMEM)
    vmem = pl.BlockSpec(memory_space=pltpu.VMEM)
    return pl.pallas_call(
        functools.partial(kernel, n_mode, n_space, count, slab),
        out_shape=jax.ShapeDtypeStruct((count, PARTNERS, slab, ny, nz), jnp.float32),
        in_specs=[smem, smem, smem, vmem, vmem],
        out_specs=vmem,
        scratch_shapes=[
            pltpu.VMEM((PARTNERS, count, wide) + plane, modes.dtype),
            pltpu.VMEM((wide,) + plane, ids.dtype),
            pltpu.VMEM((count, wide - 2) + plane, jnp.float32),
            pltpu.VMEM((count, wide - 2) + plane, jnp.float32),
            pltpu.VMEM((wide - 2,) + plane, jnp.float32),
            pltpu.VMEM((wide - 2,) + plane, jnp.float32),
            pltpu.VMEM((wide - 4,) + plane, jnp.float32),
            pltpu.VMEM((slab,) + plane, jnp.float32),
            pltpu.VMEM((wide - 6, 6) + plane, jnp.float32),
            pltpu.VMEM((slab, 3) + plane, jnp.float32),
            pltpu.VMEM((2 * nz, nz), jnp.bfloat16),
            pltpu.VMEM((ny, 2 * ny), jnp.bfloat16),
            pltpu.VMEM((3, PARTNERS, count, slab) + plane, jnp.float32),
            pltpu.VMEM((MOMENTS, padded, nz), jnp.float32),
            pltpu.VMEM((8, padded), jnp.float32),
            pltpu.VMEM((n_space, 8, padded), jnp.float32),
            pltpu.VMEM((3, padded, padded), jnp.float32),
            pltpu.SemaphoreType.DMA((2,)),
            pltpu.SemaphoreType.DMA((PARTNERS,)),
            pltpu.SemaphoreType.DMA((PARTNERS,)),
            pltpu.SemaphoreType.DMA((PARTNERS + 1, 2, depth)),
            pltpu.SemaphoreType.DMA((PARTNERS + 1, 2, depth)),
            pltpu.SemaphoreType.DMA((n_space,)),
            pltpu.SemaphoreType.DMA((n_space,)),
        ],
        compiler_params=pltpu.CompilerParams(
            collective_id=0, has_side_effects=True, vmem_limit_bytes=52 * 1024 * 1024
        ),
    )(plan, stiffness, nonlinear, modes, ids)


def coefficients(m):
    zero = jnp.zeros_like(m[0])
    one = jnp.ones_like(m[0])

    def form(left, right, at):
        total = zero
        for i in range(3):
            for j in range(3):
                if left[i] is not None and right[j] is not None:
                    total = total + left[i] * right[j] * m[i + j + at]
        return total

    z = [one, None, None]
    p = [one, None, None]
    x = [zero, zero, zero]
    rz = m[0]
    for step in range(3):
        alpha = rz / (form(p, p, 0) - form(p, p, 1))
        x = [x[i] if p[i] is None else x[i] + alpha * p[i] for i in range(3)]
        if step == 2:
            break
        old = z
        z = []
        for i in range(3):
            change = zero if p[i] is None else p[i]
            if i > 0 and p[i - 1] is not None:
                change = change - p[i - 1]
            if i > step + 1:
                z.append(None)
            else:
                z.append((zero if old[i] is None else old[i]) - alpha * change)
        new = form(z, z, 0)
        ratio = new / rz
        p = [None if z[i] is None else z[i] + (ratio * p[i] if p[i] is not None else 0.0) for i in range(3)]
        rz = new
    return x


def solution(mesh):
    return jax.shard_map(
        functools.partial(shards, mesh.shape["mode"], mesh.shape["space"]),
        mesh=mesh,
        in_specs=(
            P("mode", "space", None, None),
            P("space", None, None),
            P(),
            P(),
            P("mode", None),
        ),
        out_specs=P("mode", None, "space", None, None),
        check_vma=False,
    )
```

```python
import functools
import jax
import jax.numpy as jnp
from jax import lax
from jax.experimental import pallas as pl
from jax.experimental.pallas import tpu as pltpu
from jax.sharding import PartitionSpec as P

PARTNERS = 3
SUBS = 2
CHUNKS = 4
MASS = 0.5
LEFT = 4
RIGHT = 5
MOMENTS = 6
MESH = pl.DeviceIdType.MESH


def hops_of(reach, slab):
    found = []
    done = 0
    while done < reach:
        take = min(slab, reach - done)
        found.append((done, take))
        done += take
    return found


def shifts(v):
    rows, lanes = v.shape
    return (
        pltpu.roll(v, 1, 0),
        pltpu.roll(v, rows - 1, 0),
        pltpu.roll(v, 1, 1),
        pltpu.roll(v, lanes - 1, 1),
    )


def edge_masks(shape):
    row = lax.broadcasted_iota(jnp.int32, shape, 0)
    lane = lax.broadcasted_iota(jnp.int32, shape, 1)
    return (row > 0, row < shape[0] - 1, lane > 0, lane < shape[1] - 1)


def stencil_matrix(size, middle):
    row = lax.broadcasted_iota(jnp.int32, (size, size), 0)
    column = lax.broadcasted_iota(jnp.int32, (size, size), 1)
    beside = jnp.logical_or(row == column + 1, column == row + 1)
    return jnp.where(row == column, middle, jnp.where(beside, -1.0, 0.0)).astype(jnp.bfloat16)


def dot(left, right):
    return jnp.dot(left, right, preferred_element_type=jnp.float32)


def kernel(
    n_mode, n_space, count, slab,
    plan_ref, stiff_ref, cubic_ref, modes_ref, ids_ref,
    out_ref,
    ext_ref, idx_ref, lap_own, lap_any, coeff, g_ref, dinv, diag_own, scaled, faces,
    lanes_mat, rows_mat, basis_ref, mom_ref, sums_ref, slots, coef_ref,
    own_sem, ms, mr, zs, zr, ss, rs,
):
    mine = lax.axis_index("mode")
    place = lax.axis_index("space")
    shape = ext_ref.shape[-2:]
    wide = LEFT + slab + RIGHT
    layers = n_space * slab
    base = place * slab - LEFT
    right_hops = hops_of(LEFT, slab)
    left_hops = hops_of(RIGHT, slab)

    barrier = pltpu.get_barrier_semaphore()
    for by in range(1, n_space):
        pl.semaphore_signal(barrier, inc=1, device_id=(mine, lax.rem(place + by, n_space)), device_id_type=MESH)
    for by in (1, 2, n_mode - 2, n_mode - 1):
        pl.semaphore_signal(barrier, inc=1, device_id=(lax.rem(mine + by, n_mode), place), device_id_type=MESH)
    pl.semaphore_wait(barrier, n_space - 1 + 4)

    def z_copy(group, toward_right, hop, sub):
        done, take = (right_hops if toward_right else left_hops)[hop]
        if toward_right:
            dst = LEFT - done - take
            src = dst + slab
            target = place + 1
        else:
            dst = LEFT + slab + done
            src = dst - slab
            target = place - 1
        if group == PARTNERS:
            src_ref, dst_ref = idx_ref.at[pl.ds(src, take)], idx_ref.at[pl.ds(dst, take)]
            if hop == 0:
                src_ref = ids_ref.at[pl.ds(src - LEFT, take)]
        else:
            some = pl.ds(sub * part, part)
            src_ref, dst_ref = ext_ref.at[group, some, pl.ds(src, take)], ext_ref.at[group, some, pl.ds(dst, take)]
            if group == 0 and hop == 0:
                src_ref = modes_ref.at[some, pl.ds(src - LEFT, take)]
        side = 0 if toward_right else 1
        return pltpu.make_async_remote_copy(
            src_ref=src_ref,
            dst_ref=dst_ref,
            send_sem=zs.at[group, side, hop, sub],
            recv_sem=zr.at[group, side, hop, sub],
            device_id=(mine, jnp.clip(target, 0, n_space - 1)),
            device_id_type=MESH,
        )

    def sends(toward_right, hop):
        if toward_right:
            return jnp.logical_and(place < n_space - 1, place >= hop)
        return jnp.logical_and(place > 0, place + hop <= n_space - 1)

    def receives(toward_right, hop):
        if toward_right:
            return place >= hop + 1
        return place + hop + 1 <= n_space - 1

    def block_copy(step):
        return pltpu.make_async_remote_copy(
            src_ref=modes_ref,
            dst_ref=ext_ref.at[step, :, pl.ds(LEFT, slab)],
            send_sem=ms.at[step],
            recv_sem=mr.at[step],
            device_id=(lax.rem(mine + step, n_mode), place),
            device_id_type=MESH,
        )

    part = count // SUBS

    def each(group, hop, sub, act):
        for toward_right, hops in ((True, right_hops), (False, left_hops)):
            if hop < len(hops):
                act(group, toward_right, hop, sub)

    def start(group, toward_right, hop, sub):
        @pl.when(sends(toward_right, hop))
        def _():
            z_copy(group, toward_right, hop, sub).start()

    def arrive(group, toward_right, hop, sub):
        @pl.when(receives(toward_right, hop))
        def _():
            z_copy(group, toward_right, hop, sub).wait_recv()

    def leave(group, toward_right, hop, sub):
        @pl.when(sends(toward_right, hop))
        def _():
            z_copy(group, toward_right, hop, sub).wait_send()

    depth = max(len(right_hops), len(left_hops))

    def advance(group, hop, sub):
        each(group, hop, sub, arrive)
        if hop + 1 < depth:
            each(group, hop + 1, sub, start)

    def open_block(group):
        block_copy(group).wait_recv()
        if group + 1 < PARTNERS:
            block_copy(group + 1).start()
        for sub in range(SUBS):
            each(group, 0, sub, start)

    def set_up():
        masks = edge_masks(shape)
        regions = stiff_ref.shape[0]
        for i in range(1, wide - 1):
            ids = idx_ref[i].astype(jnp.float32)
            c = jnp.zeros(shape, jnp.float32)
            g = jnp.zeros(shape, jnp.float32)
            for k in range(regions):
                hit = ids == float(k + 1)
                c = jnp.where(hit, stiff_ref[k], c)
                g = jnp.where(hit, cubic_ref[k], g)
            coeff[i - 1] = c
            g_ref[i - 1] = g
        for i in range(2, wide - 2):
            c = coeff[i - 1]
            near = [coeff[i - 2], coeff[i]]
            near += [jnp.where(keep, moved, 0.0) for moved, keep in zip(shifts(c), masks)]
            weights = [0.5 * (c + other) for other in near]
            diag = MASS + weights[0] + weights[1] + weights[2] + weights[3] + weights[4] + weights[5]
            inside_grid = jnp.logical_and(base + i >= 0, base + i < layers).astype(jnp.float32)
            inverse = inside_grid / diag
            dinv[i - 2] = inverse
            inside = [weights[0], weights[1]] + [jnp.where(keep, w, 0.0) for w, keep in zip(weights[2:], masks)]
            if 3 <= i < wide - 3:
                for k in range(6):
                    scaled[i - 3, k] = inside[k] * inverse
            if LEFT <= i < LEFT + slab:
                diag_own[i - LEFT] = diag
                faces[i - LEFT, 0] = inside[1]
                faces[i - LEFT, 1] = inside[3]
                faces[i - LEFT, 2] = inside[5]

    def lap_loop(group, first, last):
        def lap_step(j, carry):
            across = lanes_mat[: shape[1]]
            along = rows_mat[:, : shape[0]]
            raw = {i: ext_ref[group, j, i] for i in range(first - 1, last + 1)}
            plain = {i: raw[i].astype(jnp.float32) for i in raw}
            for i in range(first, last):
                out = dot(raw[i], across) + dot(along, raw[i]) - (plain[i - 1] + plain[i + 1])
                lap_any[j, i - 1] = out
                if group == 0:
                    lap_own[j, i - 1] = out * g_ref[i - 1]
            return carry

        lax.fori_loop(0, count, lap_step, 0)

    def apply(v, i):
        below, here, above = v[i - 1], v[i], v[i + 1]
        up, down, west, east = shifts(here)
        w = [scaled[i - 3, k] for k in range(6)]
        return w[0] * below + w[1] * above + w[2] * up + w[3] * down + w[4] * west + w[5] * east

    def field_loop(s, first, last):
        def field_step(a, carry):
            j = plan_ref[a, s]
            prod, v0, v1, v2 = {}, {}, {}, {}
            sums = [None] * MOMENTS

            def add(k, value):
                sums[k] = value if sums[k] is None else sums[k] + value

            def own(i):
                return LEFT <= i < LEFT + slab

            for i in range(1, wide + 5):
                if i < wide - 1:
                    prod[i] = lap_own[a, i - 1] * lap_any[j, i - 1]
                e = i - 1
                if 2 <= e < wide - 2:
                    high = prod[e].astype(jnp.bfloat16)
                    low = (prod[e] - high.astype(jnp.float32)).astype(jnp.bfloat16)
                    rhs = prod[e - 1] + prod[e + 1]
                    rhs = rhs - dot(jnp.concatenate([high, low], 1), lanes_mat[...])
                    rhs = rhs - dot(rows_mat[...], jnp.concatenate([high, low], 0))
                    v0[e] = rhs * dinv[e - 2]
                    if own(e):
                        basis_ref[0, s, a, e - LEFT] = v0[e]
                        add(0, rhs * v0[e])
                e = i - 2
                if 3 <= e < wide - 3:
                    v1[e] = apply(v0, e)
                    if own(e):
                        basis_ref[1, s, a, e - LEFT] = v1[e]
                        heavy = diag_own[e - LEFT] * v1[e]
                        add(1, heavy * v0[e])
                        add(2, heavy * v1[e])
                e = i - 3
                if LEFT <= e < wide - 4:
                    v2[e] = apply(v1, e)
                    if own(e):
                        basis_ref[2, s, a, e - LEFT] = v2[e]
                        heavy = diag_own[e - LEFT] * v2[e]
                        add(3, heavy * v1[e])
                        add(4, heavy * v2[e])
                e = i - 4
                if own(e):
                    here = v2[e]
                    up, down, west, east = shifts(here)
                    flow = faces[e - LEFT, 0] * v2[e + 1] + faces[e - LEFT, 1] * down + faces[e - LEFT, 2] * east
                    add(5, 2.0 * (flow * here))
            for k in range(MOMENTS):
                mom_ref[k, pl.ds(s * count + a, 1), :] = jnp.sum(sums[k], axis=0, keepdims=True)
            return carry

        lax.fori_loop(first, last, field_step, 0)

    own = pltpu.make_async_copy(modes_ref, ext_ref.at[0, :, pl.ds(LEFT, slab)], own_sem.at[0])
    own_ids = pltpu.make_async_copy(ids_ref, idx_ref.at[pl.ds(LEFT, slab)], own_sem.at[1])
    each(PARTNERS, 0, 0, start)
    for sub in range(SUBS):
        each(0, 0, sub, start)
    block_copy(1).start()
    own.start()
    own_ids.start()
    for i in list(range(LEFT)) + list(range(LEFT + slab, wide)):
        @pl.when(base + i < 0 if i < LEFT else base + i >= layers)
        def _():
            idx_ref[i] = jnp.zeros(shape, idx_ref.dtype)

            def clear(j, carry):
                for group in range(PARTNERS):
                    ext_ref[group, j, i] = jnp.zeros(shape, ext_ref.dtype)
                return carry

            lax.fori_loop(0, count, clear, 0)
    lanes_mat[...] = jnp.concatenate([stencil_matrix(shape[1], 6.0)] * 2, 0)
    rows_mat[...] = jnp.concatenate([stencil_matrix(shape[0], 0.0)] * 2, 1)
    mom_ref[...] = jnp.zeros_like(mom_ref)
    own.wait()
    own_ids.wait()

    ahead = wide - 1 - left_hops[-1][1] if depth > 1 else 1
    for hop in range(depth):
        advance(PARTNERS, hop, 0)
        if hop == depth - 1:
            open_block(1)
            set_up()
            lap_loop(0, 1, ahead)
        for sub in range(SUBS):
            advance(0, hop, sub)
    lap_loop(0, ahead, wide - 1)
    bounds = [count * k // CHUNKS for k in range(CHUNKS + 1)]
    for group in range(PARTNERS):
        events = []
        if group + 1 < PARTNERS:
            for hop in range(depth - 1):
                for sub in range(SUBS):
                    events.append((hop, sub))
        if not events:
            field_loop(group, 0, count)
            continue
        for k in range(CHUNKS):
            field_loop(group, bounds[k], bounds[k + 1])
            for hop, sub in events[len(events) * k // CHUNKS : len(events) * (k + 1) // CHUNKS]:
                advance(group + 1, hop, sub)
            if k == CHUNKS // 2 - 1 and group + 2 < PARTNERS:
                open_block(group + 2)
        lap_loop(group + 1, 1, ahead)
        for sub in range(SUBS):
            advance(group + 1, depth - 1, sub)
        lap_loop(group + 1, ahead, wide - 1)

    ones = jnp.ones((8, shape[1]), jnp.float32)
    rows = []
    for k in range(MOMENTS):
        rows.append(
            lax.dot_general(
                ones, mom_ref[k], (((1,), (1,)), ((), ())),
                precision=lax.Precision.HIGHEST, preferred_element_type=jnp.float32,
            )[:1]
        )
    rows.append(jnp.zeros((8 - MOMENTS, mom_ref.shape[1]), jnp.float32))
    sums_ref[...] = jnp.concatenate(rows, 0)
    copies = []
    for by in range(1, n_space):
        copy = pltpu.make_async_remote_copy(
            src_ref=sums_ref,
            dst_ref=slots.at[by],
            send_sem=ss.at[by],
            recv_sem=rs.at[by],
            device_id=(mine, lax.rem(place + by, n_space)),
            device_id_type=MESH,
        )
        copy.start()
        copies.append(copy)
    total = sums_ref[...]
    for by in range(1, n_space):
        copies[by - 1].wait_recv()
        total = total + slots[by]
    found = coefficients([total[k : k + 1] for k in range(MOMENTS)])
    for k in range(3):
        coef_ref[k] = jnp.transpose(jnp.broadcast_to(found[k], coef_ref.shape[1:]))

    for s in range(PARTNERS):
        def combine(a, carry):
            c = [coef_ref[k, pl.ds(s * count + a, 1), :] for k in range(3)]
            for i in range(slab):
                out_ref[a, s, i] = (
                    c[0] * basis_ref[0, s, a, i] + c[1] * basis_ref[1, s, a, i] + c[2] * basis_ref[2, s, a, i]
                )
            return carry

        lax.fori_loop(0, count, combine, 0)

    for copy in copies:
        copy.wait_send()
    for step in range(1, PARTNERS):
        block_copy(step).wait_send()
    for group in range(PARTNERS + 1):
        for hop in range(depth):
            for sub in range(SUBS if group < PARTNERS else 1):
                each(group, hop, sub, leave)


def shards(n_mode, n_space, modes, regions, stiffness, nonlinear, plan):
    count, slab, ny, nz = modes.shape
    ids = (regions + 1).astype(jnp.bfloat16)
    wide = LEFT + slab + RIGHT
    depth = max(len(hops_of(LEFT, slab)), len(hops_of(RIGHT, slab)))
    padded = -(-PARTNERS * count // nz) * nz
    plane = (ny, nz)
    smem = pl.BlockSpec(memory_space=pltpu.SMEM)
    vmem = pl.BlockSpec(memory_space=pltpu.VMEM)
    return pl.pallas_call(
        functools.partial(kernel, n_mode, n_space, count, slab),
        out_shape=jax.ShapeDtypeStruct((count, PARTNERS, slab, ny, nz), jnp.float32),
        in_specs=[smem, smem, smem, vmem, vmem],
        out_specs=vmem,
        scratch_shapes=[
            pltpu.VMEM((PARTNERS, count, wide) + plane, modes.dtype),
            pltpu.VMEM((wide,) + plane, ids.dtype),
            pltpu.VMEM((count, wide - 2) + plane, jnp.float32),
            pltpu.VMEM((count, wide - 2) + plane, jnp.float32),
            pltpu.VMEM((wide - 2,) + plane, jnp.float32),
            pltpu.VMEM((wide - 2,) + plane, jnp.float32),
            pltpu.VMEM((wide - 4,) + plane, jnp.float32),
            pltpu.VMEM((slab,) + plane, jnp.float32),
            pltpu.VMEM((wide - 6, 6) + plane, jnp.float32),
            pltpu.VMEM((slab, 3) + plane, jnp.float32),
            pltpu.VMEM((2 * nz, nz), jnp.bfloat16),
            pltpu.VMEM((ny, 2 * ny), jnp.bfloat16),
            pltpu.VMEM((3, PARTNERS, count, slab) + plane, jnp.float32),
            pltpu.VMEM((MOMENTS, padded, nz), jnp.float32),
            pltpu.VMEM((8, padded), jnp.float32),
            pltpu.VMEM((n_space, 8, padded), jnp.float32),
            pltpu.VMEM((3, padded, padded), jnp.float32),
            pltpu.SemaphoreType.DMA((2,)),
            pltpu.SemaphoreType.DMA((PARTNERS,)),
            pltpu.SemaphoreType.DMA((PARTNERS,)),
            pltpu.SemaphoreType.DMA((PARTNERS + 1, 2, depth, SUBS)),
            pltpu.SemaphoreType.DMA((PARTNERS + 1, 2, depth, SUBS)),
            pltpu.SemaphoreType.DMA((n_space,)),
            pltpu.SemaphoreType.DMA((n_space,)),
        ],
        compiler_params=pltpu.CompilerParams(
            collective_id=0, has_side_effects=True, vmem_limit_bytes=52 * 1024 * 1024
        ),
    )(plan, stiffness, nonlinear, modes, ids)


def coefficients(m):
    zero = jnp.zeros_like(m[0])
    one = jnp.ones_like(m[0])

    def form(left, right, at):
        total = zero
        for i in range(3):
            for j in range(3):
                if left[i] is not None and right[j] is not None:
                    total = total + left[i] * right[j] * m[i + j + at]
        return total

    z = [one, None, None]
    p = [one, None, None]
    x = [zero, zero, zero]
    rz = m[0]
    for step in range(3):
        alpha = rz / (form(p, p, 0) - form(p, p, 1))
        x = [x[i] if p[i] is None else x[i] + alpha * p[i] for i in range(3)]
        if step == 2:
            break
        old = z
        z = []
        for i in range(3):
            change = zero if p[i] is None else p[i]
            if i > 0 and p[i - 1] is not None:
                change = change - p[i - 1]
            if i > step + 1:
                z.append(None)
            else:
                z.append((zero if old[i] is None else old[i]) - alpha * change)
        new = form(z, z, 0)
        ratio = new / rz
        p = [None if z[i] is None else z[i] + (ratio * p[i] if p[i] is not None else 0.0) for i in range(3)]
        rz = new
    return x


def solution(mesh):
    return jax.shard_map(
        functools.partial(shards, mesh.shape["mode"], mesh.shape["space"]),
        mesh=mesh,
        in_specs=(
            P("mode", "space", None, None),
            P("space", None, None),
            P(),
            P(),
            P("mode", None),
        ),
        out_specs=P("mode", None, "space", None, None),
        check_vma=False,
    )
```
